32 devices in a mesh: groups: 2 (over x), loop: 8 (over z, y), hid: 2 (over core).
Axes of the slice: x: 2, y: 2, z: 4, core: 2. Of those that a mesh axis runs over, the one named last changes fastest.
Arguments:
- tokens: bfloat16 [2048, 3072], P(('groups', 'loop')), parts along dimension 0, may hold values from -6 to 6
- cotangent: bfloat16 [2048, 3072], P(('groups', 'loop')), parts along dimension 0, may hold values from -6 to 6
- route_ids: int32 [16, 2], P('groups'), parts along dimension 0, may hold values from 0 to 7, as said below
- combine: float32 [2048], P(('groups', 'loop')), parts along dimension 0, may hold values from 0.1 to 1
- w_gate: bfloat16 [3072, 2048], P(None, ('loop', 'hid')), may hold values from -0.109375 to 0.109375
- w_up: bfloat16 [3072, 2048], P(None, ('loop', 'hid')), may hold values from -0.109375 to 0.109375
- w_down_t: bfloat16 [3072, 2048], P(None, ('loop', 'hid')), may hold values from -0.125 to 0.125
Outputs:
- mixed: bfloat16 [2048, 3072], P(('groups', 'loop'), 'hid'), parts along dimension 0
- tokens_grad: bfloat16 [2048, 3072], P(('groups', 'loop'), 'hid'), parts along dimension 0
The draws below stay inside these ranges and needn't reach their ends.
There are 2 independent parts, one for each index of `groups`. The reference program is written for one: setup_inputs(seed, part) draws one part's arguments, and reference() takes and returns one part's arrays. A program takes and returns all parts, laid end to end along the dimension named above; an argument that names none is the same for every part. Nothing has to cross between parts.
Inputs may be any that keep to these rules, and one draw needn't show every extreme that they name: `route_ids`: each row names two different experts.
All inputs are finite; a program needn't handle non-finite values.
Results may differ from the reference program's by a relative error of at most 0.012.
Values may be sent and summed in bfloat16 or wider, within the bound.
A program may use at most 128 MiB of HBM per device.

```python
import math
import jax
import jax.numpy as jnp
from jax import lax

D = 3072
FF_DEV = 128
EXPERTS = 8
BLOCK = 128
NBLK = 8
TOKENS = 1024
FF = 2048
CLASSES = 8


def draw_route_ids(key, part):
    keys = jax.random.split(key, 4)
    pick = jax.random.randint(keys[0], (NBLK,), 0, 2)
    first = jax.random.randint(keys[1], (NBLK,), 1, EXPERTS)
    offset = jax.random.randint(keys[2], (NBLK,), 1, EXPERTS - 1)
    second = 1 + (first - 1 + offset) % (EXPERTS - 1)
    flip = jax.random.randint(keys[3], (NBLK,), 0, 2)
    leading = jnp.where(pick == 0, 0, first)
    trailing = jnp.where(pick == 0, first, second)
    left = jnp.where(flip == 0, leading, trailing)
    right = jnp.where(flip == 0, trailing, leading)
    return jnp.stack([left, right], axis=1).astype(jnp.int32)


def block_scale(stream_key, extent, cuts, low, largest):
    def one(position, shards_of):
        heights = jax.random.uniform(jax.random.fold_in(jax.random.fold_in(stream_key, 6), position), (shards_of,), jnp.float32, low / len(cuts), largest / len(cuts))
        return jnp.repeat(jnp.exp(heights), extent[position] // shards_of).reshape((-1,) + (1,) * (len(extent) - position - 1))

    level = one(*cuts[0])
    for cut in cuts[1:]:
        level = level * one(*cut)
    return level


def centred(own_key, shape, deviation, most, cuts=(), held_as=jnp.bfloat16):
    level = block_scale(own_key, shape, cuts, -0.22, 0.18) if cuts else 1.0
    drawn = jax.random.normal(own_key, shape, jnp.float32) * deviation * level
    return jnp.minimum(jnp.maximum(drawn, -most), most).astype(held_as)


def setup_inputs(seed: int = 0, part: int = 0) -> dict:
    splits = jax.random.split(jax.random.key(seed), 8)
    part_keys = jax.random.split(jax.random.fold_in(splits[7], part), 8)
    tokens = centred(part_keys[0], (TOKENS, D), 1.0, 6.0, ((0, 8),))
    cotangent = centred(part_keys[1], (TOKENS, D), 1.0, 6.0, ((0, 8),))
    route_ids = draw_route_ids(jax.random.fold_in(jax.random.fold_in(splits[7], part), 71), part)
    combine = jnp.clip(jnp.exp(math.log(1.0) - 2.3025851 * jax.random.uniform(part_keys[3], (TOKENS,), jnp.float32) ** block_scale(part_keys[3], (TOKENS,), ((0, 8),), -0.2, 0.2)), 0.1, 1.0)
    w_gate = centred(splits[4], (D, FF), D ** -0.5, 0.109375, ((1, 16),))
    w_up = centred(splits[5], (D, FF), D ** -0.5, 0.109375, ((1, 16),))
    w_down_t = centred(splits[6], (D, FF), FF ** -0.5, 0.125, ((1, 16),))
    return {"tokens": tokens, "cotangent": cotangent, "route_ids": route_ids, "combine": combine, "w_gate": w_gate, "w_up": w_up, "w_down_t": w_down_t}


def class_major(matrix):
    rows = matrix.shape[0]
    folded = matrix.reshape(rows, -1, CLASSES, FF_DEV)
    return jnp.transpose(folded, (2, 0, 1, 3)).reshape(CLASSES, rows, -1)


def rounded_total(parts):
    rounded = lax.optimization_barrier(parts.astype(jnp.bfloat16))
    return jnp.sum(rounded.astype(jnp.float32), axis=0)


def reference(tokens, cotangent, route_ids, combine, w_gate, w_up, w_down_t):
    routed = jnp.any(route_ids == 0, axis=1)
    row_weight = combine * jnp.repeat(routed.astype(jnp.float32), BLOCK)
    block_count = tokens.shape[0] // BLOCK
    width = tokens.shape[1]
    token_blocks = tokens.reshape(block_count, BLOCK, width)
    cotangent_blocks = cotangent.reshape(block_count, BLOCK, width)
    weight_blocks = row_weight.reshape(block_count, BLOCK)
    gate_classes = class_major(w_gate)
    up_classes = class_major(w_up)
    down_classes = class_major(w_down_t)

    def one_block(item):
        inputs, cotan, weight, flag = item

        def compute(operand):
            gate = jnp.dot(inputs, w_gate, preferred_element_type=jnp.float32)
            upward = jnp.dot(inputs, w_up, preferred_element_type=jnp.float32)
            sigma = jax.nn.sigmoid(gate)
            active = gate * sigma
            hidden = (active * upward).astype(jnp.bfloat16)
            hidden_classes = class_major(hidden)

            def out_part(pair):
                return jnp.dot(pair[0], pair[1].T, preferred_element_type=jnp.float32)

            summed = rounded_total(lax.map(out_part, (hidden_classes, down_classes)))
            mixed = (weight[:, None] * summed).astype(jnp.bfloat16)
            scaled = (weight[:, None] * cotan.astype(jnp.float32)).astype(jnp.bfloat16)
            grad_hidden = jnp.dot(scaled, w_down_t, preferred_element_type=jnp.float32)
            grad_gate = (grad_hidden * upward * sigma * (1.0 + gate * (1.0 - sigma))).astype(jnp.bfloat16)
            grad_up = (grad_hidden * active).astype(jnp.bfloat16)

            def in_part(quad):
                first = jnp.dot(quad[0], quad[1].T, preferred_element_type=jnp.float32)
                return first + jnp.dot(quad[2], quad[3].T, preferred_element_type=jnp.float32)

            total = rounded_total(lax.map(in_part, (class_major(grad_gate), gate_classes, class_major(grad_up), up_classes)))
            return mixed, total.astype(jnp.bfloat16)

        def nothing(operand):
            zeros = jnp.zeros((BLOCK, width), jnp.bfloat16)
            return zeros, zeros

        return lax.cond(flag, compute, nothing, 0)

    mixed, grads = lax.map(one_block, (token_blocks, cotangent_blocks, weight_blocks, routed))
    return mixed.reshape(tokens.shape), grads.reshape(tokens.shape)
```

```python
import functools

import jax
import jax.numpy as jnp
from jax import lax
from jax.experimental import pallas as pl
from jax.experimental.pallas import tpu as pltpu
from jax.sharding import PartitionSpec as P

BLOCK = 128
PARTS_OF_WEIGHT = 2
MESH = pl.DeviceIdType.MESH


def line_kernel(
    line, route_ref, combine_ref, tokens_ref, cotangent_ref, gate_ref, up_ref, down_ref,
    mixed_ref, grad_ref,
    weights, rows_in, cotan, hidden, sums, from_left, from_right, total, swap_out, swap_in,
    own_sem, gather_send, gather_recv,
    sibling_send, sibling_recv, side_send, side_recv, cross_send, cross_recv,
    relay_send, relay_recv, left_send, left_recv, right_recv, swap_send, swap_recv,
):
    group = lax.axis_index("groups")
    loop = lax.axis_index("loop")
    core = lax.axis_index("hid")
    place = loop // 2
    half = rows_in.shape[2]
    width = rows_in.shape[3]
    units = gate_ref.shape[1]
    chunk = width // 2
    sibling = {"hid": 1 - core}
    side = {"loop": loop + 1 - 2 * lax.rem(loop, 2)}
    cross = {"groups": 1 - group}
    left = {"loop": loop - 2}
    right = {"loop": loop + 2}
    has_left = place > 0
    has_right = place < line - 1
    sources = (gate_ref, up_ref, down_ref)
    my_rows = pl.ds(pl.multiple_of(core * half, half), half)

    barrier = pltpu.get_barrier_semaphore()
    for other in (sibling, side, cross):
        pl.semaphore_signal(barrier, inc=1, device_id=other, device_id_type=MESH)

    @pl.when(has_left)
    def _():
        pl.semaphore_signal(barrier, inc=1, device_id=left, device_id_type=MESH)

    @pl.when(has_right)
    def _():
        pl.semaphore_signal(barrier, inc=1, device_id=right, device_id_type=MESH)

    own = [
        pltpu.make_async_copy(cotangent_ref.at[my_rows, :], cotan, own_sem.at[0]),
        pltpu.make_async_copy(tokens_ref.at[my_rows, :], rows_in.at[place, 0], own_sem.at[1]),
    ]
    for m in range(3):
        own.append(
            pltpu.make_async_copy(sources[m], weights.at[m, :, pl.ds(0, units)], own_sem.at[2 + m])
        )
    for copy in own:
        copy.start()

    @pl.when(has_left & has_right)
    def _():
        pl.semaphore_wait(barrier, 5)

    @pl.when(jnp.logical_not(has_left & has_right))
    def _():
        pl.semaphore_wait(barrier, 4)

    def remote(src, dst, send, recv, other):
        return pltpu.make_async_remote_copy(
            src_ref=src, dst_ref=dst, send_sem=send, recv_sem=recv,
            device_id=other, device_id_type=MESH,
        )

    def gather_copy(block, kind, way):
        other = left if way == 0 else right
        ref = rows_in.at[block, kind]
        return remote(
            ref, ref, gather_send.at[way, block, kind], gather_recv.at[block, kind], other
        )

    def send_both(kind):
        @pl.when(has_left)
        def _():
            gather_copy(place, kind, 0).start()

        @pl.when(has_right)
        def _():
            gather_copy(place, kind, 1).start()

    piece = width // 2 // PARTS_OF_WEIGHT

    def piece_rows(part_half, i):
        return pl.ds(pl.multiple_of(part_half * (width // 2) + i * piece, piece), piece)

    def side_copy(m, i):
        rows = piece_rows(group, i)
        return remote(
            sources[m].at[rows, :], weights.at[m, rows, pl.ds(2 * units, units)],
            side_send.at[m, i], side_recv.at[m, i], side,
        )

    def cross_copy(m, i, part_half):
        ref = weights.at[m, piece_rows(part_half, i), pl.ds(2 * units, units)]
        return remote(ref, ref, cross_send.at[m, i], cross_recv.at[m, i], cross)

    def relay_copy(m, i, late):
        rows = piece_rows(group if late == 0 else 1 - group, i)
        return remote(
            weights.at[m, rows, pl.ds(2 * units, units)],
            weights.at[m, rows, pl.ds(3 * units, units)],
            relay_send.at[late, m, i], relay_recv.at[late, m, i], sibling,
        )

    def sibling_copy(m):
        return remote(
            sources[m], weights.at[m, :, pl.ds(units, units)],
            sibling_send.at[m], sibling_recv.at[m], sibling,
        )

    for m in range(3):
        for i in range(PARTS_OF_WEIGHT):
            side_copy(m, i).start()
    own[1].wait()
    send_both(0)

    chosen = (route_ref[loop, 0] == 0) | (route_ref[loop, 1] == 0)
    flag = jnp.where(chosen, 1.0, 0.0)
    lanes = lax.broadcasted_iota(jnp.int32, (half, 2 * half), 1)
    heights = lax.broadcasted_iota(jnp.int32, (half, 2 * half), 0) + core * half
    picked = jnp.where(lanes == heights, combine_ref[...], 0.0)
    row_weight = jnp.sum(picked, axis=1, keepdims=True) * flag
    own[0].wait()
    rows_in[place, 1] = (row_weight * cotan[...].astype(jnp.float32)).astype(jnp.bfloat16)
    send_both(1)
    for m in range(3):
        sibling_copy(m).start()

    def pass_on(distance, kind):
        @pl.when((place - distance >= 0) & has_right)
        def _():
            gather_copy(place - distance, kind, 1).wait_recv()
            gather_copy(place - distance, kind, 1).start()

        @pl.when((place + distance < line) & has_left)
        def _():
            gather_copy(place + distance, kind, 0).wait_recv()
            gather_copy(place + distance, kind, 0).start()

    relays = [(d, kind) for d in range(1, line - 1) for kind in range(2)]
    pieces = [(m, i) for m in range(3) for i in range(PARTS_OF_WEIGHT)]
    for step, (m, i) in enumerate(pieces):
        side_copy(m, i).wait_recv()
        cross_copy(m, i, group).start()
        relay_copy(m, i, 0).start()
        if step % 2 == 1 and relays:
            pass_on(*relays.pop(0))
        if step >= 1:
            mm, ii = pieces[step - 1]
            cross_copy(mm, ii, 1 - group).wait_recv()
            relay_copy(mm, ii, 1).start()
    mm, ii = pieces[-1]
    cross_copy(mm, ii, 1 - group).wait_recv()
    relay_copy(mm, ii, 1).start()
    while relays:
        pass_on(*relays.pop(0))
    for m in range(3):
        own[2 + m].wait()
        sibling_copy(m).wait_recv()
        for i in range(PARTS_OF_WEIGHT):
            relay_copy(m, i, 0).wait_recv()
            relay_copy(m, i, 1).wait_recv()

    contract = (((1,), (1,)), ((), ()))

    def terms(block):
        def first(t, _):
            cols = pl.ds(pl.multiple_of(t * 256, 256), 256)
            gate = jnp.dot(rows_in[block, 0], weights[0, :, cols], preferred_element_type=jnp.float32)
            upward = jnp.dot(rows_in[block, 0], weights[1, :, cols], preferred_element_type=jnp.float32)
            grad_hidden = jnp.dot(
                rows_in[block, 1], weights[2, :, cols], preferred_element_type=jnp.float32
            )
            sigma = jax.nn.sigmoid(gate)
            active = gate * sigma
            hidden[0, :, cols] = (active * upward).astype(jnp.bfloat16)
            hidden[1, :, cols] = (
                grad_hidden * upward * sigma * (1.0 + gate * (1.0 - sigma))
            ).astype(jnp.bfloat16)
            hidden[2, :, cols] = (grad_hidden * active).astype(jnp.bfloat16)
            return 0

        lax.fori_loop(0, weights.shape[2] // 256, first, 0)

        def second(t, _):
            cols = pl.ds(pl.multiple_of(t * 512, 512), 512)
            output_part = lax.dot_general(
                hidden[0], weights[2, cols, :], contract, preferred_element_type=jnp.float32
            )
            sums[block, 0, :, cols] = output_part.astype(jnp.bfloat16)
            input_part = lax.dot_general(
                hidden[1], weights[0, cols, :], contract, preferred_element_type=jnp.float32
            ) + lax.dot_general(
                hidden[2], weights[1, cols, :], contract, preferred_element_type=jnp.float32
            )
            sums[block, 1, :, cols] = input_part.astype(jnp.bfloat16)
            return 0

        lax.fori_loop(0, width // 512, second, 0)

    def sum_copy(block, kind, part, way):
        cols = pl.ds(part * chunk, chunk)
        target = from_right if way == 0 else from_left
        recv = right_recv if way == 0 else left_recv
        return remote(
            sums.at[block, kind, :, cols], target.at[block, kind, :, cols],
            left_send.at[block, kind, part], recv.at[block, kind, part],
            left if way == 0 else right,
        )

    quarters = [(kind, part) for kind in range(2) for part in range(2)]

    def one_block(index, _):
        distance = (index + 2) // 2
        way = lax.rem(index, 2)
        apart = jnp.where(index == 2 * (line - 1), 0, distance * (2 * way - 1))
        block = place + apart

        @pl.when((block >= 0) & (block < line))
        def _():
            @pl.when(jnp.logical_not(has_left) & (apart > 0))
            def _():
                for kind in range(2):
                    gather_copy(block, kind, 0).wait_recv()

            @pl.when(jnp.logical_not(has_right) & (apart < 0))
            def _():
                for kind in range(2):
                    gather_copy(block, kind, 1).wait_recv()

            terms(block)

            @pl.when(jnp.logical_not(has_left) & (apart > 0))
            def _():
                for kind, part in quarters:
                    sum_copy(block, kind, part, 1).start()

            @pl.when(jnp.logical_not(has_right) & (apart < 0))
            def _():
                for kind, part in quarters:
                    sum_copy(block, kind, part, 0).start()

        return 0

    lax.fori_loop(0, 2 * (line - 1) + 1, one_block, 0)

    def merge(block, kind, part, arrived):
        cols = pl.ds(part * chunk, chunk)
        sums[block, kind, :, cols] = (
            sums[block, kind, :, cols].astype(jnp.float32)
            + arrived[block, kind, :, cols].astype(jnp.float32)
        ).astype(jnp.bfloat16)

    def forward(block, kind, part, way):
        sum_copy(block, kind, part, way).wait_recv()
        merge(block, kind, part, from_left if way == 1 else from_right)
        sum_copy(block, kind, part, way).start()

    low = place < line // 2

    def onward(turn, _):
        to_right = has_left & (turn > place)
        to_left = has_right & (line - 1 - turn < place)
        for kind, part in quarters:
            @pl.when(to_right & low)
            def _():
                forward(turn, kind, part, 1)

            @pl.when(to_left)
            def _():
                forward(line - 1 - turn, kind, part, 0)

            @pl.when(to_right & jnp.logical_not(low))
            def _():
                forward(turn, kind, part, 1)
        return 0

    lax.fori_loop(1, line, onward, 0)

    outputs = (mixed_ref, grad_ref)

    def swap_copy(kind):
        return remote(
            swap_out.at[kind], swap_in.at[kind], swap_send.at[kind], swap_recv.at[kind], sibling
        )

    for kind in range(2):
        for part in range(2):
            cols = pl.ds(part * chunk, chunk)
            total[...] = sums[place, kind, :, cols].astype(jnp.float32)

            @pl.when(has_left)
            def _():
                sum_copy(place, kind, part, 1).wait_recv()
                total[...] += from_left[place, kind, :, cols].astype(jnp.float32)

            @pl.when(has_right)
            def _():
                sum_copy(place, kind, part, 0).wait_recv()
                total[...] += from_right[place, kind, :, cols].astype(jnp.float32)

            value = total[...]
            if kind == 0:
                value = row_weight * value
            value = value.astype(jnp.bfloat16)

            @pl.when(core == part)
            def _():
                outputs[kind][my_rows, :] = value

            @pl.when(core != part)
            def _():
                swap_out[kind] = value
        swap_copy(kind).start()
    other_rows = pl.ds(pl.multiple_of((1 - core) * half, half), half)
    for kind in range(2):
        swap_copy(kind).wait_recv()
        outputs[kind][other_rows, :] = swap_in[kind]

    for kind in range(2):
        swap_copy(kind).wait_send()
    for m in range(3):
        sibling_copy(m).wait_send()
        for i in range(PARTS_OF_WEIGHT):
            side_copy(m, i).wait_send()
            cross_copy(m, i, group).wait_send()
            relay_copy(m, i, 0).wait_send()
            relay_copy(m, i, 1).wait_send()

    def settle(block, _):
        @pl.when(has_left & (block >= place))
        def _():
            for kind in range(2):
                gather_copy(block, kind, 0).wait_send()

        @pl.when(has_right & (block <= place))
        def _():
            for kind in range(2):
                gather_copy(block, kind, 1).wait_send()

        @pl.when(block != place)
        def _():
            for kind, part in quarters:
                sum_copy(block, kind, part, 0).wait_send()
        return 0

    lax.fori_loop(0, line, settle, 0)


def on_line(tokens, cotangent, route_ids, combine, w_gate, w_up, w_down_t):
    rows, width = tokens.shape
    units = w_gate.shape[1]
    half = rows // 2
    line = lax.axis_size("loop") // 2
    any_space = pl.BlockSpec(memory_space=pl.ANY)
    vmem = pl.BlockSpec(memory_space=pltpu.VMEM)
    bf16 = jnp.bfloat16
    dma = pltpu.SemaphoreType.DMA
    pieces = PARTS_OF_WEIGHT
    out = jax.ShapeDtypeStruct((rows, width // 2), bf16)
    return pl.pallas_call(
        functools.partial(line_kernel, line),
        out_shape=(out, out),
        in_specs=[pl.BlockSpec(memory_space=pltpu.SMEM), vmem] + [any_space] * 5,
        out_specs=(vmem, vmem),
        scratch_shapes=[
            pltpu.VMEM((3, width, 4 * units), bf16),
            pltpu.VMEM((line, 2, half, width), bf16),
            pltpu.VMEM((half, width), bf16),
            pltpu.VMEM((3, half, 4 * units), bf16),
            pltpu.VMEM((line, 2, half, width), bf16),
            pltpu.VMEM((line, 2, half, width), bf16),
            pltpu.VMEM((line, 2, half, width), bf16),
            pltpu.VMEM((half, width // 2), jnp.float32),
            pltpu.VMEM((2, half, width // 2), bf16),
            pltpu.VMEM((2, half, width // 2), bf16),
            dma((5,)),
            dma((2, line, 2)),
            dma((line, 2)),
            dma((3,)),
            dma((3,)),
            dma((3, pieces)),
            dma((3, pieces)),
            dma((3, pieces)),
            dma((3, pieces)),
            dma((2, 3, pieces)),
            dma((2, 3, pieces)),
            dma((line, 2, 2)),
            dma((line, 2, 2)),
            dma((line, 2, 2)),
            dma((2,)),
            dma((2,)),
        ],
        compiler_params=pltpu.CompilerParams(
            collective_id=0, has_side_effects=True, vmem_limit_bytes=48 * 1024 * 1024
        ),
        cost_estimate=pl.CostEstimate(
            flops=12 * line * half * width * 4 * units,
            bytes_accessed=2 * (3 * width * units + 3 * rows * width),
            transcendentals=line * half * 4 * units,
        ),
    )(route_ids, combine.reshape(1, rows), tokens, cotangent, w_gate, w_up, w_down_t)


def from_partner(block, axis, distance):
    count = lax.axis_size(axis)
    route = []
    for low in range(count):
        high = low | 1 << distance
        if high != low and high < count:
            route += [(low, high), (high, low)]
    return lax.ppermute(block, axis, route)


def from_behind(block, axis, distance):
    devices = range(lax.axis_size(axis))
    route = [((i - distance) % len(devices), i) for i in devices]
    return lax.ppermute(block, axis, route)


def block_terms(stacked_weights, group_rows, routed_group, totals):
    weight_gate = stacked_weights[0]
    weight_up = stacked_weights[1]
    weight_down = stacked_weights[2]
    contract = (((1,), (1,)), ((), ()))

    def one_block(position, state):

        def compute(current):
            start = position * BLOCK
            inputs = lax.dynamic_slice_in_dim(group_rows[0], start, BLOCK, 0)
            scaled = lax.dynamic_slice_in_dim(group_rows[1], start, BLOCK, 0)
            gate = jnp.dot(inputs, weight_gate, preferred_element_type=jnp.float32)
            upward = jnp.dot(inputs, weight_up, preferred_element_type=jnp.float32)
            sigma = jax.nn.sigmoid(gate)
            active = gate * sigma
            hidden = (active * upward).astype(jnp.bfloat16)
            output_part = lax.dot_general(
                hidden, weight_down, contract, preferred_element_type=jnp.float32
            )
            grad_hidden = jnp.dot(scaled, weight_down, preferred_element_type=jnp.float32)
            grad_gate = (grad_hidden * upward * sigma * (1.0 + gate * (1.0 - sigma))).astype(
                jnp.bfloat16
            )
            grad_up = (grad_hidden * active).astype(jnp.bfloat16)
            input_part = lax.dot_general(
                grad_gate, weight_gate, contract, preferred_element_type=jnp.float32
            )
            input_part = input_part + lax.dot_general(
                grad_up, weight_up, contract, preferred_element_type=jnp.float32
            )
            previous = lax.dynamic_slice_in_dim(current, start, BLOCK, 1)
            return lax.dynamic_update_slice_in_dim(
                current, previous + jnp.stack([output_part, input_part]), start, 1
            )

        def keep_state(current):
            return current

        return lax.cond(routed_group[position] > 0, compute, keep_state, state)

    return lax.fori_loop(0, routed_group.shape[0], one_block, totals)


def split_halves(values, loop_index, bit):
    half_rows = values.shape[1] // 2
    upper_bit = loop_index >> bit & 1
    lower_part = values[:, :half_rows]
    upper_part = values[:, half_rows:]
    kept = jnp.where(upper_bit == 0, lower_part, upper_part)
    outgoing = jnp.where(upper_bit == 0, upper_part, lower_part)
    return (kept, outgoing)


def on_device(tokens, cotangent, route_ids, combine, w_gate, w_up, w_down_t):
    row_count = tokens.shape[0]
    blocks_here = row_count // BLOCK
    loop_index = lax.axis_index("loop")
    cycle_size = lax.axis_size("loop")
    routed = jnp.any(route_ids == 0, axis=1).astype(jnp.int32)
    local_routed = lax.dynamic_slice_in_dim(routed, loop_index * blocks_here, blocks_here)
    row_weight = combine * jnp.repeat(local_routed.astype(jnp.float32), BLOCK)
    scaled = (row_weight[:, None] * cotangent.astype(jnp.float32)).astype(jnp.bfloat16)
    group_rows = jnp.stack([tokens, scaled])
    for bit in range(2):
        partner = from_partner(group_rows, "loop", bit)
        upper_bit = loop_index >> bit & 1
        group_rows = jnp.where(
            upper_bit == 0,
            jnp.concatenate([group_rows, partner], 1),
            jnp.concatenate([partner, group_rows], 1),
        )
    group_start = loop_index // 4 * 4 * blocks_here
    routed_group = lax.dynamic_slice_in_dim(routed, group_start, 4 * blocks_here)
    totals = jnp.zeros((2, 4 * row_count, tokens.shape[1]), jnp.float32)
    weights = jnp.stack([w_gate, w_up, w_down_t])
    turns = cycle_size // 4

    def turn_once(step, carry):
        current, sums = carry
        sums = block_terms(current, group_rows, routed_group, sums)
        current = from_behind(current, "loop", 4)
        return (current, sums)

    weights, totals = lax.fori_loop(0, turns - 1, turn_once, (weights, totals))
    totals = block_terms(weights, group_rows, routed_group, totals)
    rounded = totals.astype(jnp.bfloat16)
    kept, outgoing = split_halves(rounded, loop_index, 1)
    received = from_partner(outgoing, "loop", 1)
    sums = kept.astype(jnp.float32) + received.astype(jnp.float32)
    kept, outgoing = split_halves(sums, loop_index, 0)
    sums = kept + from_partner(outgoing.astype(jnp.bfloat16), "loop", 0).astype(outgoing.dtype)
    sums = lax.psum_scatter(
        sums.astype(jnp.bfloat16), "hid", scatter_dimension=2, tiled=True
    ).astype(jnp.float32)
    mixed = (row_weight[:, None] * sums[0]).astype(jnp.bfloat16)
    tokens_grad = sums[1].astype(jnp.bfloat16)
    return (mixed, tokens_grad)


def solution(mesh):
    in_specs = (
        P(("groups", "loop"), None),
        P(("groups", "loop"), None),
        P("groups", None),
        P(("groups", "loop")),
        P(None, ("loop", "hid")),
        P(None, ("loop", "hid")),
        P(None, ("loop", "hid")),
    )
    out_specs = (P(("groups", "loop"), "hid"), P(("groups", "loop"), "hid"))
    sizes = dict(mesh.shape)
    short = sizes["groups"] == 2 and sizes["hid"] == 2 and sizes["loop"] == 8
    return jax.shard_map(
        on_line if short else on_device, mesh=mesh, in_specs=in_specs, out_specs=out_specs, check_vma=False
    )
```

```python
import functools

import jax
import jax.numpy as jnp
from jax import lax
from jax.experimental import pallas as pl
from jax.experimental.pallas import tpu as pltpu
from jax.sharding import PartitionSpec as P

BLOCK = 128
PARTS_OF_WEIGHT = 2
MESH = pl.DeviceIdType.MESH


def line_kernel(
    line, route_ref, combine_ref, tokens_ref, cotangent_ref, gate_ref, up_ref, down_ref,
    mixed_ref, grad_ref,
    weights, rows_in, cotan, hidden, sums, arrived, total, swap_out, swap_in,
    own_sem, gather_send, gather_recv,
    sibling_send, sibling_recv, side_send, side_recv, cross_send, cross_recv,
    relay_send, relay_recv, sums_send, sums_recv, swap_send, swap_recv,
):
    group = lax.axis_index("groups")
    loop = lax.axis_index("loop")
    core = lax.axis_index("hid")
    place = loop // 2
    half = rows_in.shape[2]
    width = rows_in.shape[3]
    units = gate_ref.shape[1]
    chunk = width // 2
    sibling = {"hid": 1 - core}
    side = {"loop": loop + 1 - 2 * lax.rem(loop, 2)}
    cross = {"groups": 1 - group}
    left = {"loop": loop - 2}
    right = {"loop": loop + 2}
    has_left = place > 0
    has_right = place < line - 1
    sources = (gate_ref, up_ref, down_ref)
    my_rows = pl.ds(pl.multiple_of(core * half, half), half)

    barrier = pltpu.get_barrier_semaphore()
    for other in (sibling, side, cross):
        pl.semaphore_signal(barrier, inc=1, device_id=other, device_id_type=MESH)

    @pl.when(has_left)
    def _():
        pl.semaphore_signal(barrier, inc=1, device_id=left, device_id_type=MESH)

    @pl.when(has_right)
    def _():
        pl.semaphore_signal(barrier, inc=1, device_id=right, device_id_type=MESH)

    own = [
        pltpu.make_async_copy(cotangent_ref.at[my_rows, :], cotan, own_sem.at[0]),
        pltpu.make_async_copy(tokens_ref.at[my_rows, :], rows_in.at[place, 0], own_sem.at[1]),
    ]
    for m in range(3):
        own.append(
            pltpu.make_async_copy(sources[m], weights.at[m, :, pl.ds(0, units)], own_sem.at[2 + m])
        )
    for copy in own:
        copy.start()

    @pl.when(has_left & has_right)
    def _():
        pl.semaphore_wait(barrier, 5)

    @pl.when(jnp.logical_not(has_left & has_right))
    def _():
        pl.semaphore_wait(barrier, 4)

    def remote(src, dst, send, recv, other):
        return pltpu.make_async_remote_copy(
            src_ref=src, dst_ref=dst, send_sem=send, recv_sem=recv,
            device_id=other, device_id_type=MESH,
        )

    def gather_copy(block, kind, way):
        other = left if way == 0 else right
        ref = rows_in.at[block, kind]
        return remote(
            ref, ref, gather_send.at[way, block, kind], gather_recv.at[block, kind], other
        )

    def send_both(kind):
        @pl.when(has_left)
        def _():
            gather_copy(place, kind, 0).start()

        @pl.when(has_right)
        def _():
            gather_copy(place, kind, 1).start()

    piece = width // 2 // PARTS_OF_WEIGHT

    def piece_rows(part_half, i):
        return pl.ds(pl.multiple_of(part_half * (width // 2) + i * piece, piece), piece)

    def side_copy(m, i):
        rows = piece_rows(group, i)
        return remote(
            sources[m].at[rows, :], weights.at[m, rows, pl.ds(2 * units, units)],
            side_send.at[m, i], side_recv.at[m, i], side,
        )

    def cross_copy(m, i, part_half):
        ref = weights.at[m, piece_rows(part_half, i), pl.ds(2 * units, units)]
        return remote(ref, ref, cross_send.at[m, i], cross_recv.at[m, i], cross)

    def relay_copy(m, i, late):
        rows = piece_rows(group if late == 0 else 1 - group, i)
        return remote(
            weights.at[m, rows, pl.ds(2 * units, units)],
            weights.at[m, rows, pl.ds(3 * units, units)],
            relay_send.at[late, m, i], relay_recv.at[late, m, i], sibling,
        )

    def sibling_copy(m):
        return remote(
            sources[m], weights.at[m, :, pl.ds(units, units)],
            sibling_send.at[m], sibling_recv.at[m], sibling,
        )

    for m in range(3):
        for i in range(PARTS_OF_WEIGHT):
            side_copy(m, i).start()
    own[1].wait()
    send_both(0)

    chosen = (route_ref[loop, 0] == 0) | (route_ref[loop, 1] == 0)
    flag = jnp.where(chosen, 1.0, 0.0)
    lanes = lax.broadcasted_iota(jnp.int32, (half, 2 * half), 1)
    heights = lax.broadcasted_iota(jnp.int32, (half, 2 * half), 0) + core * half
    picked = jnp.where(lanes == heights, combine_ref[...], 0.0)
    row_weight = jnp.sum(picked, axis=1, keepdims=True) * flag
    own[0].wait()
    rows_in[place, 1] = (row_weight * cotan[...].astype(jnp.float32)).astype(jnp.bfloat16)
    send_both(1)
    for m in range(3):
        sibling_copy(m).start()

    def pass_on(distance, kind):
        @pl.when((place - distance >= 0) & has_right)
        def _():
            gather_copy(place - distance, kind, 1).wait_recv()
            gather_copy(place - distance, kind, 1).start()

        @pl.when((place + distance < line) & has_left)
        def _():
            gather_copy(place + distance, kind, 0).wait_recv()
            gather_copy(place + distance, kind, 0).start()

    relays = [(d, kind) for d in range(1, line - 1) for kind in range(2)]
    pieces = [(m, i) for m in range(3) for i in range(PARTS_OF_WEIGHT)]
    for step, (m, i) in enumerate(pieces):
        side_copy(m, i).wait_recv()
        cross_copy(m, i, group).start()
        relay_copy(m, i, 0).start()
        if step % 2 == 1 and relays:
            pass_on(*relays.pop(0))
        if step >= 1:
            mm, ii = pieces[step - 1]
            cross_copy(mm, ii, 1 - group).wait_recv()
            relay_copy(mm, ii, 1).start()
    mm, ii = pieces[-1]
    cross_copy(mm, ii, 1 - group).wait_recv()
    relay_copy(mm, ii, 1).start()
    while relays:
        pass_on(*relays.pop(0))
    for m in range(3):
        own[2 + m].wait()
        sibling_copy(m).wait_recv()
        for i in range(PARTS_OF_WEIGHT):
            relay_copy(m, i, 0).wait_recv()
            relay_copy(m, i, 1).wait_recv()

    contract = (((1,), (1,)), ((), ()))

    def terms(block, ready):
        def first(t, _):
            cols = pl.ds(pl.multiple_of(t * 256, 256), 256)
            gate = jnp.dot(rows_in[block, 0], weights[0, :, cols], preferred_element_type=jnp.float32)
            upward = jnp.dot(rows_in[block, 0], weights[1, :, cols], preferred_element_type=jnp.float32)
            grad_hidden = jnp.dot(
                rows_in[block, 1], weights[2, :, cols], preferred_element_type=jnp.float32
            )
            sigma = jax.nn.sigmoid(gate)
            active = gate * sigma
            hidden[0, :, cols] = (active * upward).astype(jnp.bfloat16)
            hidden[1, :, cols] = (
                grad_hidden * upward * sigma * (1.0 + gate * (1.0 - sigma))
            ).astype(jnp.bfloat16)
            hidden[2, :, cols] = (grad_hidden * active).astype(jnp.bfloat16)
            return 0

        lax.fori_loop(0, weights.shape[2] // 256, first, 0)

        def output_tile(t, _):
            cols = pl.ds(pl.multiple_of(t * 512, 512), 512)
            output_part = lax.dot_general(
                hidden[0], weights[2, cols, :], contract, preferred_element_type=jnp.float32
            )
            sums[block, 0, :, cols] = output_part.astype(jnp.bfloat16)
            return 0

        lax.fori_loop(0, width // 512, output_tile, 0)
        ready(0)

        def input_tile(t, _):
            cols = pl.ds(pl.multiple_of(t * 512, 512), 512)
            input_part = lax.dot_general(
                hidden[1], weights[0, cols, :], contract, preferred_element_type=jnp.float32
            ) + lax.dot_general(
                hidden[2], weights[1, cols, :], contract, preferred_element_type=jnp.float32
            )
            sums[block, 1, :, cols] = input_part.astype(jnp.bfloat16)
            return 0

        lax.fori_loop(0, width // 512, input_tile, 0)
        ready(1)

    def sum_copy(block, kind, part, way):
        cols = pl.ds(part * chunk, chunk)
        return remote(
            sums.at[block, kind, :, cols], arrived.at[way, block, kind, :, cols],
            sums_send.at[block, kind, part], sums_recv.at[way, block, kind, part],
            {"loop": loop + 4 * way - 2},
        )

    quarters = [(kind, part) for kind in range(2) for part in range(2)]
    low = place < line // 2
    at_end = jnp.logical_not(has_left & has_right)
    depth = jnp.where(low, place, line - 1 - place)
    onward_way = jnp.where(low, 1, 0)

    def mirrored(block):
        return jnp.where(low, block, line - 1 - block)

    def one_block(index, _):
        later = jnp.where(index == 2, 3 - 3 * depth, depth)
        block = mirrored(jnp.where(index == 0, 2, jnp.where(index == 1, 1 + 2 * depth, later)))

        @pl.when(at_end & (index < line - 1))
        def _():
            for kind in range(2):
                gather_copy(block, kind, 0).wait_recv()

        def ready(kind):
            @pl.when(at_end & ((index == 0) | (index == 2)))
            def _():
                for part in range(2):
                    sum_copy(block, kind, part, onward_way).start()

        terms(block, ready)

        @pl.when(at_end & (index == 2))
        def _():
            for kind, part in quarters:
                sum_copy(mirrored(1), kind, part, onward_way).start()

        return 0

    lax.fori_loop(0, line, one_block, 0)

    def forward(block, kind, part, way):
        cols = pl.ds(part * chunk, chunk)
        sum_copy(block, kind, part, way).wait_recv()
        sums[block, kind, :, cols] = (
            sums[block, kind, :, cols].astype(jnp.float32)
            + arrived[way, block, kind, :, cols].astype(jnp.float32)
        ).astype(jnp.bfloat16)
        sum_copy(block, kind, part, way).start()

    @pl.when(has_left & has_right)
    def _():
        def onward(turn, _):
            block = mirrored(jnp.where(turn == 0, 2, jnp.where(turn == 1, 3, 0)))
            way = jnp.where(turn == 2, 1 - onward_way, onward_way)
            for kind, part in quarters:
                forward(block, kind, part, way)
            return 0

        lax.fori_loop(0, 3, onward, 0)

    outputs = (mixed_ref, grad_ref)

    def swap_copy(kind):
        return remote(
            swap_out.at[kind], swap_in.at[kind], swap_send.at[kind], swap_recv.at[kind], sibling
        )

    for kind in range(2):
        for part in range(2):
            cols = pl.ds(part * chunk, chunk)
            total[...] = sums[place, kind, :, cols].astype(jnp.float32)

            @pl.when(has_left)
            def _():
                sum_copy(place, kind, part, 1).wait_recv()
                total[...] += arrived[1, place, kind, :, cols].astype(jnp.float32)

            @pl.when(has_right)
            def _():
                sum_copy(place, kind, part, 0).wait_recv()
                total[...] += arrived[0, place, kind, :, cols].astype(jnp.float32)

            value = total[...]
            if kind == 0:
                value = row_weight * value
            value = value.astype(jnp.bfloat16)

            @pl.when(core == part)
            def _():
                outputs[kind][my_rows, :] = value

            @pl.when(core != part)
            def _():
                swap_out[kind] = value
        swap_copy(kind).start()
    other_rows = pl.ds(pl.multiple_of((1 - core) * half, half), half)
    for kind in range(2):
        swap_copy(kind).wait_recv()
        outputs[kind][other_rows, :] = swap_in[kind]

    for kind in range(2):
        swap_copy(kind).wait_send()
    for m in range(3):
        sibling_copy(m).wait_send()
        for i in range(PARTS_OF_WEIGHT):
            side_copy(m, i).wait_send()
            cross_copy(m, i, group).wait_send()
            relay_copy(m, i, 0).wait_send()
            relay_copy(m, i, 1).wait_send()

    def settle(block, _):
        @pl.when(has_left & (block >= place))
        def _():
            for kind in range(2):
                gather_copy(block, kind, 0).wait_send()

        @pl.when(has_right & (block <= place))
        def _():
            for kind in range(2):
                gather_copy(block, kind, 1).wait_send()

        @pl.when(block != place)
        def _():
            for kind, part in quarters:
                sum_copy(block, kind, part, 0).wait_send()
        return 0

    lax.fori_loop(0, line, settle, 0)


def on_line(tokens, cotangent, route_ids, combine, w_gate, w_up, w_down_t):
    rows, width = tokens.shape
    units = w_gate.shape[1]
    half = rows // 2
    line = lax.axis_size("loop") // 2
    any_space = pl.BlockSpec(memory_space=pltpu.HBM)
    vmem = pl.BlockSpec(memory_space=pltpu.VMEM)
    bf16 = jnp.bfloat16
    dma = pltpu.SemaphoreType.DMA
    pieces = PARTS_OF_WEIGHT
    out = jax.ShapeDtypeStruct((rows, width // 2), bf16)
    return pl.pallas_call(
        functools.partial(line_kernel, line),
        out_shape=(out, out),
        in_specs=[pl.BlockSpec(memory_space=pltpu.SMEM), vmem] + [any_space] * 5,
        out_specs=(vmem, vmem),
        scratch_shapes=[
            pltpu.VMEM((3, width, 4 * units), bf16),
            pltpu.VMEM((line, 2, half, width), bf16),
            pltpu.VMEM((half, width), bf16),
            pltpu.VMEM((3, half, 4 * units), bf16),
            pltpu.VMEM((line, 2, half, width), bf16),
            pltpu.VMEM((2, line, 2, half, width), bf16),
            pltpu.VMEM((half, width // 2), jnp.float32),
            pltpu.VMEM((2, half, width // 2), bf16),
            pltpu.VMEM((2, half, width // 2), bf16),
            dma((5,)),
            dma((2, line, 2)),
            dma((line, 2)),
            dma((3,)),
            dma((3,)),
            dma((3, pieces)),
            dma((3, pieces)),
            dma((3, pieces)),
            dma((3, pieces)),
            dma((2, 3, pieces)),
            dma((2, 3, pieces)),
            dma((line, 2, 2)),
            dma((2, line, 2, 2)),
            dma((2,)),
            dma((2,)),
        ],
        compiler_params=pltpu.CompilerParams(
            collective_id=0, has_side_effects=True, vmem_limit_bytes=62 * 1024 * 1024
        ),
        cost_estimate=pl.CostEstimate(
            flops=12 * line * half * width * 4 * units,
            bytes_accessed=2 * (3 * width * units + 3 * rows * width),
            transcendentals=line * half * 4 * units,
        ),
    )(route_ids, combine.reshape(1, rows), tokens, cotangent, w_gate, w_up, w_down_t)


def from_partner(block, axis, distance):
    count = lax.axis_size(axis)
    route = []
    for low in range(count):
        high = low | 1 << distance
        if high != low and high < count:
            route += [(low, high), (high, low)]
    return lax.ppermute(block, axis, route)


def from_behind(block, axis, distance):
    devices = range(lax.axis_size(axis))
    route = [((i - distance) % len(devices), i) for i in devices]
    return lax.ppermute(block, axis, route)


def block_terms(stacked_weights, group_rows, routed_group, totals):
    weight_gate = stacked_weights[0]
    weight_up = stacked_weights[1]
    weight_down = stacked_weights[2]
    contract = (((1,), (1,)), ((), ()))

    def one_block(position, state):

        def compute(current):
            start = position * BLOCK
            inputs = lax.dynamic_slice_in_dim(group_rows[0], start, BLOCK, 0)
            scaled = lax.dynamic_slice_in_dim(group_rows[1], start, BLOCK, 0)
            gate = jnp.dot(inputs, weight_gate, preferred_element_type=jnp.float32)
            upward = jnp.dot(inputs, weight_up, preferred_element_type=jnp.float32)
            sigma = jax.nn.sigmoid(gate)
            active = gate * sigma
            hidden = (active * upward).astype(jnp.bfloat16)
            output_part = lax.dot_general(
                hidden, weight_down, contract, preferred_element_type=jnp.float32
            )
            grad_hidden = jnp.dot(scaled, weight_down, preferred_element_type=jnp.float32)
            grad_gate = (grad_hidden * upward * sigma * (1.0 + gate * (1.0 - sigma))).astype(
                jnp.bfloat16
            )
            grad_up = (grad_hidden * active).astype(jnp.bfloat16)
            input_part = lax.dot_general(
                grad_gate, weight_gate, contract, preferred_element_type=jnp.float32
            )
            input_part = input_part + lax.dot_general(
                grad_up, weight_up, contract, preferred_element_type=jnp.float32
            )
            previous = lax.dynamic_slice_in_dim(current, start, BLOCK, 1)
            return lax.dynamic_update_slice_in_dim(
                current, previous + jnp.stack([output_part, input_part]), start, 1
            )

        def keep_state(current):
            return current

        return lax.cond(routed_group[position] > 0, compute, keep_state, state)

    return lax.fori_loop(0, routed_group.shape[0], one_block, totals)


def split_halves(values, loop_index, bit):
    half_rows = values.shape[1] // 2
    upper_bit = loop_index >> bit & 1
    lower_part = values[:, :half_rows]
    upper_part = values[:, half_rows:]
    kept = jnp.where(upper_bit == 0, lower_part, upper_part)
    outgoing = jnp.where(upper_bit == 0, upper_part, lower_part)
    return (kept, outgoing)


def on_device(tokens, cotangent, route_ids, combine, w_gate, w_up, w_down_t):
    row_count = tokens.shape[0]
    blocks_here = row_count // BLOCK
    loop_index = lax.axis_index("loop")
    cycle_size = lax.axis_size("loop")
    routed = jnp.any(route_ids == 0, axis=1).astype(jnp.int32)
    local_routed = lax.dynamic_slice_in_dim(routed, loop_index * blocks_here, blocks_here)
    row_weight = combine * jnp.repeat(local_routed.astype(jnp.float32), BLOCK)
    scaled = (row_weight[:, None] * cotangent.astype(jnp.float32)).astype(jnp.bfloat16)
    group_rows = jnp.stack([tokens, scaled])
    for bit in range(2):
        partner = from_partner(group_rows, "loop", bit)
        upper_bit = loop_index >> bit & 1
        group_rows = jnp.where(
            upper_bit == 0,
            jnp.concatenate([group_rows, partner], 1),
            jnp.concatenate([partner, group_rows], 1),
        )
    group_start = loop_index // 4 * 4 * blocks_here
    routed_group = lax.dynamic_slice_in_dim(routed, group_start, 4 * blocks_here)
    totals = jnp.zeros((2, 4 * row_count, tokens.shape[1]), jnp.float32)
    weights = jnp.stack([w_gate, w_up, w_down_t])
    turns = cycle_size // 4

    def turn_once(step, carry):
        current, sums = carry
        sums = block_terms(current, group_rows, routed_group, sums)
        current = from_behind(current, "loop", 4)
        return (current, sums)

    weights, totals = lax.fori_loop(0, turns - 1, turn_once, (weights, totals))
    totals = block_terms(weights, group_rows, routed_group, totals)
    rounded = totals.astype(jnp.bfloat16)
    kept, outgoing = split_halves(rounded, loop_index, 1)
    received = from_partner(outgoing, "loop", 1)
    sums = kept.astype(jnp.float32) + received.astype(jnp.float32)
    kept, outgoing = split_halves(sums, loop_index, 0)
    sums = kept + from_partner(outgoing.astype(jnp.bfloat16), "loop", 0).astype(outgoing.dtype)
    sums = lax.psum_scatter(
        sums.astype(jnp.bfloat16), "hid", scatter_dimension=2, tiled=True
    ).astype(jnp.float32)
    mixed = (row_weight[:, None] * sums[0]).astype(jnp.bfloat16)
    tokens_grad = sums[1].astype(jnp.bfloat16)
    return (mixed, tokens_grad)


def solution(mesh):
    in_specs = (
        P(("groups", "loop"), None),
        P(("groups", "loop"), None),
        P("groups", None),
        P(("groups", "loop")),
        P(None, ("loop", "hid")),
        P(None, ("loop", "hid")),
        P(None, ("loop", "hid")),
    )
    out_specs = (P(("groups", "loop"), "hid"), P(("groups", "loop"), "hid"))
    sizes = dict(mesh.shape)
    short = sizes["groups"] == 2 and sizes["hid"] == 2 and sizes["loop"] == 8
    return jax.shard_map(
        on_line if short else on_device, mesh=mesh, in_specs=in_specs, out_specs=out_specs, check_vma=False
    )
```

```python
import functools

import jax
import jax.numpy as jnp
from jax import lax
from jax.experimental import pallas as pl
from jax.experimental.pallas import tpu as pltpu
from jax.sharding import PartitionSpec as P

BLOCK = 128
PARTS_OF_WEIGHT = 2
MESH = pl.DeviceIdType.MESH


def line_kernel(
    line, route_ref, combine_ref, tokens_ref, cotangent_ref, gate_ref, up_ref, down_ref,
    mixed_ref, grad_ref,
    weights, rows_in, cotan, hidden, sums, arrived, total, swap_out, swap_in,
    own_sem, gather_send, gather_recv,
    sibling_send, sibling_recv, side_send, side_recv, cross_send, cross_recv,
    relay_send, relay_recv, sums_send, sums_recv, swap_send, swap_recv,
):
    group = lax.axis_index("groups")
    loop = lax.axis_index("loop")
    core = lax.axis_index("hid")
    place = loop // 2
    half = rows_in.shape[2]
    width = rows_in.shape[3]
    units = gate_ref.shape[1]
    chunk = width // 2
    sibling = {"hid": 1 - core}
    side = {"loop": loop + 1 - 2 * lax.rem(loop, 2)}
    cross = {"groups": 1 - group}
    left = {"loop": loop - 2}
    right = {"loop": loop + 2}
    has_left = place > 0
    has_right = place < line - 1
    sources = (gate_ref, up_ref, down_ref)
    my_rows = pl.ds(pl.multiple_of(core * half, half), half)

    barrier = pltpu.get_barrier_semaphore()
    for other in (sibling, side, cross):
        pl.semaphore_signal(barrier, inc=1, device_id=other, device_id_type=MESH)

    @pl.when(has_left)
    def _():
        pl.semaphore_signal(barrier, inc=1, device_id=left, device_id_type=MESH)

    @pl.when(has_right)
    def _():
        pl.semaphore_signal(barrier, inc=1, device_id=right, device_id_type=MESH)

    own = [
        pltpu.make_async_copy(cotangent_ref.at[my_rows, :], cotan, own_sem.at[0]),
        pltpu.make_async_copy(tokens_ref.at[my_rows, :], rows_in.at[place, 0], own_sem.at[1]),
    ]
    for m in range(3):
        own.append(
            pltpu.make_async_copy(sources[m], weights.at[m, :, pl.ds(0, units)], own_sem.at[2 + m])
        )
    for copy in own:
        copy.start()

    @pl.when(has_left & has_right)
    def _():
        pl.semaphore_wait(barrier, 5)

    @pl.when(jnp.logical_not(has_left & has_right))
    def _():
        pl.semaphore_wait(barrier, 4)

    def remote(src, dst, send, recv, other):
        return pltpu.make_async_remote_copy(
            src_ref=src, dst_ref=dst, send_sem=send, recv_sem=recv,
            device_id=other, device_id_type=MESH,
        )

    def gather_copy(block, kind, way):
        other = left if way == 0 else right
        ref = rows_in.at[block, kind]
        return remote(
            ref, ref, gather_send.at[way, block, kind], gather_recv.at[block, kind], other
        )

    def send_both(kind):
        @pl.when(has_left)
        def _():
            gather_copy(place, kind, 0).start()

        @pl.when(has_right)
        def _():
            gather_copy(place, kind, 1).start()

    piece = width // 2 // PARTS_OF_WEIGHT

    def piece_rows(part_half, i):
        return pl.ds(pl.multiple_of(part_half * (width // 2) + i * piece, piece), piece)

    def side_copy(m, i):
        rows = piece_rows(group, i)
        return remote(
            sources[m].at[rows, :], weights.at[m, rows, pl.ds(2 * units, units)],
            side_send.at[m, i], side_recv.at[m, i], side,
        )

    def cross_copy(m, i, part_half):
        ref = weights.at[m, piece_rows(part_half, i), pl.ds(2 * units, units)]
        return remote(ref, ref, cross_send.at[m, i], cross_recv.at[m, i], cross)

    def relay_copy(m, i, late):
        rows = piece_rows(group if late == 0 else 1 - group, i)
        return remote(
            weights.at[m, rows, pl.ds(2 * units, units)],
            weights.at[m, rows, pl.ds(3 * units, units)],
            relay_send.at[late, m, i], relay_recv.at[late, m, i], sibling,
        )

    def sibling_copy(m):
        return remote(
            sources[m], weights.at[m, :, pl.ds(units, units)],
            sibling_send.at[m], sibling_recv.at[m], sibling,
        )

    for m in range(3):
        for i in range(PARTS_OF_WEIGHT):
            side_copy(m, i).start()
    own[1].wait()
    send_both(0)

    chosen = (route_ref[loop, 0] == 0) | (route_ref[loop, 1] == 0)
    flag = jnp.where(chosen, 1.0, 0.0)
    lanes = lax.broadcasted_iota(jnp.int32, (half, 2 * half), 1)
    heights = lax.broadcasted_iota(jnp.int32, (half, 2 * half), 0) + core * half
    picked = jnp.where(lanes == heights, combine_ref[...], 0.0)
    row_weight = jnp.sum(picked, axis=1, keepdims=True) * flag
    own[0].wait()
    rows_in[place, 1] = (row_weight * cotan[...].astype(jnp.float32)).astype(jnp.bfloat16)
    send_both(1)
    for m in range(3):
        sibling_copy(m).start()

    def pass_on(distance, kind):
        @pl.when((place - distance >= 0) & has_right)
        def _():
            gather_copy(place - distance, kind, 1).wait_recv()
            gather_copy(place - distance, kind, 1).start()

        @pl.when((place + distance < line) & has_left)
        def _():
            gather_copy(place + distance, kind, 0).wait_recv()
            gather_copy(place + distance, kind, 0).start()

    relays = [(d, kind) for d in range(1, line - 1) for kind in range(2)]
    pieces = [(m, i) for m in range(3) for i in range(PARTS_OF_WEIGHT)]
    for step, (m, i) in enumerate(pieces):
        side_copy(m, i).wait_recv()
        cross_copy(m, i, group).start()
        relay_copy(m, i, 0).start()
        if step % 2 == 1 and relays:
            pass_on(*relays.pop(0))
        if step >= 1:
            mm, ii = pieces[step - 1]
            cross_copy(mm, ii, 1 - group).wait_recv()
            relay_copy(mm, ii, 1).start()
    mm, ii = pieces[-1]
    cross_copy(mm, ii, 1 - group).wait_recv()
    relay_copy(mm, ii, 1).start()
    while relays:
        pass_on(*relays.pop(0))
    for m in range(3):
        own[2 + m].wait()
        sibling_copy(m).wait_recv()
        for i in range(PARTS_OF_WEIGHT):
            relay_copy(m, i, 0).wait_recv()
            relay_copy(m, i, 1).wait_recv()

    contract = (((1,), (1,)), ((), ()))

    def terms(blocks, ready):
        def first(t, _):
            cols = pl.ds(pl.multiple_of(t * 256, 256), 256)
            inputs = jnp.concatenate([rows_in[b, 0] for b in blocks], axis=0)
            scaled = jnp.concatenate([rows_in[b, 1] for b in blocks], axis=0)
            gate = jnp.dot(inputs, weights[0, :, cols], preferred_element_type=jnp.float32)
            upward = jnp.dot(inputs, weights[1, :, cols], preferred_element_type=jnp.float32)
            grad_hidden = jnp.dot(scaled, weights[2, :, cols], preferred_element_type=jnp.float32)
            sigma = jax.nn.sigmoid(gate)
            active = gate * sigma
            hidden[0, :, cols] = (active * upward).astype(jnp.bfloat16)
            hidden[1, :, cols] = (
                grad_hidden * upward * sigma * (1.0 + gate * (1.0 - sigma))
            ).astype(jnp.bfloat16)
            hidden[2, :, cols] = (grad_hidden * active).astype(jnp.bfloat16)
            return 0

        lax.fori_loop(0, weights.shape[2] // 256, first, 0)

        def keep(kind, cols, value):
            for i, b in enumerate(blocks):
                sums[b, kind, :, cols] = value[i * half:(i + 1) * half].astype(jnp.bfloat16)

        def output_tile(t, _):
            cols = pl.ds(pl.multiple_of(t * 512, 512), 512)
            keep(0, cols, lax.dot_general(
                hidden[0], weights[2, cols, :], contract, preferred_element_type=jnp.float32
            ))
            return 0

        lax.fori_loop(0, width // 512, output_tile, 0)
        ready(0)

        def input_tile(t, _):
            cols = pl.ds(pl.multiple_of(t * 512, 512), 512)
            keep(1, cols, lax.dot_general(
                hidden[1], weights[0, cols, :], contract, preferred_element_type=jnp.float32
            ) + lax.dot_general(
                hidden[2], weights[1, cols, :], contract, preferred_element_type=jnp.float32
            ))
            return 0

        lax.fori_loop(0, width // 512, input_tile, 0)
        ready(1)

    def sum_copy(block, kind, part, way):
        cols = pl.ds(part * chunk, chunk)
        return remote(
            sums.at[block, kind, :, cols], arrived.at[way, block, kind, :, cols],
            sums_send.at[block, kind, part], sums_recv.at[way, block, kind, part],
            {"loop": loop + 4 * way - 2},
        )

    quarters = [(kind, part) for kind in range(2) for part in range(2)]
    low = place < line // 2
    at_end = jnp.logical_not(has_left & has_right)
    depth = jnp.where(low, place, line - 1 - place)
    onward_way = jnp.where(low, 1, 0)

    def mirrored(block):
        return jnp.where(low, block, line - 1 - block)

    def forward(block, kind, part, way):
        cols = pl.ds(part * chunk, chunk)
        sum_copy(block, kind, part, way).wait_recv()
        sums[block, kind, :, cols] = (
            sums[block, kind, :, cols].astype(jnp.float32)
            + arrived[way, block, kind, :, cols].astype(jnp.float32)
        ).astype(jnp.bfloat16)
        sum_copy(block, kind, part, way).start()

    def two_blocks(index, _):
        ahead = mirrored(jnp.where(index == 0, 2, 3 - 3 * depth))
        behind = mirrored(jnp.where(index == 0, 1 + 2 * depth, depth))

        @pl.when(at_end)
        def _():
            for kind in range(2):
                gather_copy(ahead, kind, 0).wait_recv()

        @pl.when(at_end & (index == 0))
        def _():
            for kind in range(2):
                gather_copy(behind, kind, 0).wait_recv()

        def ready(kind):
            @pl.when(at_end)
            def _():
                for part in range(2):
                    sum_copy(ahead, kind, part, onward_way).start()

        terms((ahead, behind), ready)

        @pl.when(at_end & (index == 1))
        def _():
            for kind, part in quarters:
                sum_copy(mirrored(1), kind, part, onward_way).start()

        @pl.when(jnp.logical_not(at_end))
        def _():
            for part in range(2):
                forward(mirrored(2), index, part, onward_way)

        return 0

    lax.fori_loop(0, 2, two_blocks, 0)

    @pl.when(jnp.logical_not(at_end))
    def _():
        def onward(turn, _):
            block = mirrored(3 - 3 * turn)
            way = jnp.where(turn == 1, 1 - onward_way, onward_way)
            for kind, part in quarters:
                forward(block, kind, part, way)
            return 0

        lax.fori_loop(0, 2, onward, 0)

    outputs = (mixed_ref, grad_ref)

    def swap_copy(kind):
        return remote(
            swap_out.at[kind], swap_in.at[kind], swap_send.at[kind], swap_recv.at[kind], sibling
        )

    for kind in range(2):
        for part in range(2):
            cols = pl.ds(part * chunk, chunk)
            total[...] = sums[place, kind, :, cols].astype(jnp.float32)

            @pl.when(has_left)
            def _():
                sum_copy(place, kind, part, 1).wait_recv()
                total[...] += arrived[1, place, kind, :, cols].astype(jnp.float32)

            @pl.when(has_right)
            def _():
                sum_copy(place, kind, part, 0).wait_recv()
                total[...] += arrived[0, place, kind, :, cols].astype(jnp.float32)

            value = total[...]
            if kind == 0:
                value = row_weight * value
            value = value.astype(jnp.bfloat16)

            @pl.when(core == part)
            def _():
                outputs[kind][my_rows, :] = value

            @pl.when(core != part)
            def _():
                swap_out[kind] = value
        swap_copy(kind).start()
    other_rows = pl.ds(pl.multiple_of((1 - core) * half, half), half)
    for kind in range(2):
        swap_copy(kind).wait_recv()
        outputs[kind][other_rows, :] = swap_in[kind]

    for kind in range(2):
        swap_copy(kind).wait_send()
    for m in range(3):
        sibling_copy(m).wait_send()
        for i in range(PARTS_OF_WEIGHT):
            side_copy(m, i).wait_send()
            cross_copy(m, i, group).wait_send()
            relay_copy(m, i, 0).wait_send()
            relay_copy(m, i, 1).wait_send()

    def settle(block, _):
        @pl.when(has_left & (block >= place))
        def _():
            for kind in range(2):
                gather_copy(block, kind, 0).wait_send()

        @pl.when(has_right & (block <= place))
        def _():
            for kind in range(2):
                gather_copy(block, kind, 1).wait_send()

        @pl.when(block != place)
        def _():
            for kind, part in quarters:
                sum_copy(block, kind, part, 0).wait_send()
        return 0

    lax.fori_loop(0, line, settle, 0)


def on_line(tokens, cotangent, route_ids, combine, w_gate, w_up, w_down_t):
    rows, width = tokens.shape
    units = w_gate.shape[1]
    half = rows // 2
    line = lax.axis_size("loop") // 2
    any_space = pl.BlockSpec(memory_space=pltpu.HBM)
    vmem = pl.BlockSpec(memory_space=pltpu.VMEM)
    bf16 = jnp.bfloat16
    dma = pltpu.SemaphoreType.DMA
    pieces = PARTS_OF_WEIGHT
    out = jax.ShapeDtypeStruct((rows, width // 2), bf16)
    return pl.pallas_call(
        functools.partial(line_kernel, line),
        out_shape=(out, out),
        in_specs=[pl.BlockSpec(memory_space=pltpu.SMEM), vmem] + [any_space] * 5,
        out_specs=(vmem, vmem),
        scratch_shapes=[
            pltpu.VMEM((3, width, 4 * units), bf16),
            pltpu.VMEM((line, 2, half, width), bf16),
            pltpu.VMEM((half, width), bf16),
            pltpu.VMEM((3, 2 * half, 4 * units), bf16),
            pltpu.VMEM((line, 2, half, width), bf16),
            pltpu.VMEM((2, line, 2, half, width), bf16),
            pltpu.VMEM((half, width // 2), jnp.float32),
            pltpu.VMEM((2, half, width // 2), bf16),
            pltpu.VMEM((2, half, width // 2), bf16),
            dma((5,)),
            dma((2, line, 2)),
            dma((line, 2)),
            dma((3,)),
            dma((3,)),
            dma((3, pieces)),
            dma((3, pieces)),
            dma((3, pieces)),
            dma((3, pieces)),
            dma((2, 3, pieces)),
            dma((2, 3, pieces)),
            dma((line, 2, 2)),
            dma((2, line, 2, 2)),
            dma((2,)),
            dma((2,)),
        ],
        compiler_params=pltpu.CompilerParams(
            collective_id=0, has_side_effects=True, vmem_limit_bytes=62 * 1024 * 1024
        ),
        cost_estimate=pl.CostEstimate(
            flops=12 * line * half * width * 4 * units,
            bytes_accessed=2 * (3 * width * units + 3 * rows * width),
            transcendentals=line * half * 4 * units,
        ),
    )(route_ids, combine.reshape(1, rows), tokens, cotangent, w_gate, w_up, w_down_t)


def from_partner(block, axis, distance):
    count = lax.axis_size(axis)
    route = []
    for low in range(count):
        high = low | 1 << distance
        if high != low and high < count:
            route += [(low, high), (high, low)]
    return lax.ppermute(block, axis, route)


def from_behind(block, axis, distance):
    devices = range(lax.axis_size(axis))
    route = [((i - distance) % len(devices), i) for i in devices]
    return lax.ppermute(block, axis, route)


def block_terms(stacked_weights, group_rows, routed_group, totals):
    weight_gate = stacked_weights[0]
    weight_up = stacked_weights[1]
    weight_down = stacked_weights[2]
    contract = (((1,), (1,)), ((), ()))

    def one_block(position, state):

        def compute(current):
            start = position * BLOCK
            inputs = lax.dynamic_slice_in_dim(group_rows[0], start, BLOCK, 0)
            scaled = lax.dynamic_slice_in_dim(group_rows[1], start, BLOCK, 0)
            gate = jnp.dot(inputs, weight_gate, preferred_element_type=jnp.float32)
            upward = jnp.dot(inputs, weight_up, preferred_element_type=jnp.float32)
            sigma = jax.nn.sigmoid(gate)
            active = gate * sigma
            hidden = (active * upward).astype(jnp.bfloat16)
            output_part = lax.dot_general(
                hidden, weight_down, contract, preferred_element_type=jnp.float32
            )
            grad_hidden = jnp.dot(scaled, weight_down, preferred_element_type=jnp.float32)
            grad_gate = (grad_hidden * upward * sigma * (1.0 + gate * (1.0 - sigma))).astype(
                jnp.bfloat16
            )
            grad_up = (grad_hidden * active).astype(jnp.bfloat16)
            input_part = lax.dot_general(
                grad_gate, weight_gate, contract, preferred_element_type=jnp.float32
            )
            input_part = input_part + lax.dot_general(
                grad_up, weight_up, contract, preferred_element_type=jnp.float32
            )
            previous = lax.dynamic_slice_in_dim(current, start, BLOCK, 1)
            return lax.dynamic_update_slice_in_dim(
                current, previous + jnp.stack([output_part, input_part]), start, 1
            )

        def keep_state(current):
            return current

        return lax.cond(routed_group[position] > 0, compute, keep_state, state)

    return lax.fori_loop(0, routed_group.shape[0], one_block, totals)


def split_halves(values, loop_index, bit):
    half_rows = values.shape[1] // 2
    upper_bit = loop_index >> bit & 1
    lower_part = values[:, :half_rows]
    upper_part = values[:, half_rows:]
    kept = jnp.where(upper_bit == 0, lower_part, upper_part)
    outgoing = jnp.where(upper_bit == 0, upper_part, lower_part)
    return (kept, outgoing)


def on_device(tokens, cotangent, route_ids, combine, w_gate, w_up, w_down_t):
    row_count = tokens.shape[0]
    blocks_here = row_count // BLOCK
    loop_index = lax.axis_index("loop")
    cycle_size = lax.axis_size("loop")
    routed = jnp.any(route_ids == 0, axis=1).astype(jnp.int32)
    local_routed = lax.dynamic_slice_in_dim(routed, loop_index * blocks_here, blocks_here)
    row_weight = combine * jnp.repeat(local_routed.astype(jnp.float32), BLOCK)
    scaled = (row_weight[:, None] * cotangent.astype(jnp.float32)).astype(jnp.bfloat16)
    group_rows = jnp.stack([tokens, scaled])
    for bit in range(2):
        partner = from_partner(group_rows, "loop", bit)
        upper_bit = loop_index >> bit & 1
        group_rows = jnp.where(
            upper_bit == 0,
            jnp.concatenate([group_rows, partner], 1),
            jnp.concatenate([partner, group_rows], 1),
        )
    group_start = loop_index // 4 * 4 * blocks_here
    routed_group = lax.dynamic_slice_in_dim(routed, group_start, 4 * blocks_here)
    totals = jnp.zeros((2, 4 * row_count, tokens.shape[1]), jnp.float32)
    weights = jnp.stack([w_gate, w_up, w_down_t])
    turns = cycle_size // 4

    def turn_once(step, carry):
        current, sums = carry
        sums = block_terms(current, group_rows, routed_group, sums)
        current = from_behind(current, "loop", 4)
        return (current, sums)

    weights, totals = lax.fori_loop(0, turns - 1, turn_once, (weights, totals))
    totals = block_terms(weights, group_rows, routed_group, totals)
    rounded = totals.astype(jnp.bfloat16)
    kept, outgoing = split_halves(rounded, loop_index, 1)
    received = from_partner(outgoing, "loop", 1)
    sums = kept.astype(jnp.float32) + received.astype(jnp.float32)
    kept, outgoing = split_halves(sums, loop_index, 0)
    sums = kept + from_partner(outgoing.astype(jnp.bfloat16), "loop", 0).astype(outgoing.dtype)
    sums = lax.psum_scatter(
        sums.astype(jnp.bfloat16), "hid", scatter_dimension=2, tiled=True
    ).astype(jnp.float32)
    mixed = (row_weight[:, None] * sums[0]).astype(jnp.bfloat16)
    tokens_grad = sums[1].astype(jnp.bfloat16)
    return (mixed, tokens_grad)


def solution(mesh):
    in_specs = (
        P(("groups", "loop"), None),
        P(("groups", "loop"), None),
        P("groups", None),
        P(("groups", "loop")),
        P(None, ("loop", "hid")),
        P(None, ("loop", "hid")),
        P(None, ("loop", "hid")),
    )
    out_specs = (P(("groups", "loop"), "hid"), P(("groups", "loop"), "hid"))
    sizes = dict(mesh.shape)
    short = sizes["groups"] == 2 and sizes["hid"] == 2 and sizes["loop"] == 8
    return jax.shard_map(
        on_line if short else on_device, mesh=mesh, in_specs=in_specs, out_specs=out_specs, check_vma=False
    )
```

```python
import functools

import jax
import jax.numpy as jnp
from jax import lax
from jax.experimental import pallas as pl
from jax.experimental.pallas import tpu as pltpu
from jax.sharding import PartitionSpec as P

BLOCK = 128
PARTS_OF_WEIGHT = 2
MESH = pl.DeviceIdType.MESH


def line_kernel(
    line, route_ref, combine_ref, tokens_ref, cotangent_ref, gate_ref, up_ref, down_ref,
    mixed_ref, grad_ref,
    weights, rows_in, cotan, hidden, sums, arrived, total, swap_out, swap_in,
    own_sem, gather_send, gather_recv,
    sibling_send, sibling_recv, side_send, side_recv, cross_send, cross_recv,
    relay_send, relay_recv, sums_send, sums_recv, swap_send, swap_recv,
):
    group = lax.axis_index("groups")
    loop = lax.axis_index("loop")
    core = lax.axis_index("hid")
    place = loop // 2
    half = rows_in.shape[2]
    width = rows_in.shape[3]
    units = gate_ref.shape[1]
    chunk = width // 2
    sibling = {"hid": 1 - core}
    side = {"loop": loop + 1 - 2 * lax.rem(loop, 2)}
    cross = {"groups": 1 - group}
    left = {"loop": loop - 2}
    right = {"loop": loop + 2}
    has_left = place > 0
    has_right = place < line - 1
    sources = (gate_ref, up_ref, down_ref)
    my_rows = pl.ds(pl.multiple_of(core * half, half), half)

    barrier = pltpu.get_barrier_semaphore()
    for other in (sibling, side, cross):
        pl.semaphore_signal(barrier, inc=1, device_id=other, device_id_type=MESH)

    @pl.when(has_left)
    def _():
        pl.semaphore_signal(barrier, inc=1, device_id=left, device_id_type=MESH)

    @pl.when(has_right)
    def _():
        pl.semaphore_signal(barrier, inc=1, device_id=right, device_id_type=MESH)

    own = [
        pltpu.make_async_copy(cotangent_ref.at[my_rows, :], cotan, own_sem.at[0]),
        pltpu.make_async_copy(tokens_ref.at[my_rows, :], rows_in.at[place, 0], own_sem.at[1]),
    ]
    for m in range(3):
        own.append(
            pltpu.make_async_copy(sources[m], weights.at[m, :, pl.ds(0, units)], own_sem.at[2 + m])
        )
    for copy in own:
        copy.start()

    @pl.when(has_left & has_right)
    def _():
        pl.semaphore_wait(barrier, 5)

    @pl.when(jnp.logical_not(has_left & has_right))
    def _():
        pl.semaphore_wait(barrier, 4)

    def remote(src, dst, send, recv, other):
        return pltpu.make_async_remote_copy(
            src_ref=src, dst_ref=dst, send_sem=send, recv_sem=recv,
            device_id=other, device_id_type=MESH,
        )

    def gather_copy(block, kind, way):
        other = left if way == 0 else right
        ref = rows_in.at[block, kind]
        return remote(
            ref, ref, gather_send.at[way, block, kind], gather_recv.at[block, kind], other
        )

    def send_both(kind):
        @pl.when(has_left)
        def _():
            gather_copy(place, kind, 0).start()

        @pl.when(has_right)
        def _():
            gather_copy(place, kind, 1).start()

    piece = width // 2 // PARTS_OF_WEIGHT

    def piece_rows(part_half, i):
        return pl.ds(pl.multiple_of(part_half * (width // 2) + i * piece, piece), piece)

    def side_copy(m, i):
        rows = piece_rows(group, i)
        return remote(
            sources[m].at[rows, :], weights.at[m, rows, pl.ds(2 * units, units)],
            side_send.at[m, i], side_recv.at[m, i], side,
        )

    def cross_copy(m, i, part_half):
        ref = weights.at[m, piece_rows(part_half, i), pl.ds(2 * units, units)]
        return remote(ref, ref, cross_send.at[m, i], cross_recv.at[m, i], cross)

    def relay_copy(m, i, late):
        rows = piece_rows(group if late == 0 else 1 - group, i)
        return remote(
            weights.at[m, rows, pl.ds(2 * units, units)],
            weights.at[m, rows, pl.ds(3 * units, units)],
            relay_send.at[late, m, i], relay_recv.at[late, m, i], sibling,
        )

    def sibling_copy(m):
        return remote(
            sources[m], weights.at[m, :, pl.ds(units, units)],
            sibling_send.at[m], sibling_recv.at[m], sibling,
        )

    for m in range(3):
        for i in range(PARTS_OF_WEIGHT):
            side_copy(m, i).start()
    own[1].wait()
    send_both(0)

    chosen = (route_ref[loop, 0] == 0) | (route_ref[loop, 1] == 0)
    flag = jnp.where(chosen, 1.0, 0.0)
    lanes = lax.broadcasted_iota(jnp.int32, (half, 2 * half), 1)
    heights = lax.broadcasted_iota(jnp.int32, (half, 2 * half), 0) + core * half
    picked = jnp.where(lanes == heights, combine_ref[...], 0.0)
    row_weight = jnp.sum(picked, axis=1, keepdims=True) * flag
    own[0].wait()
    rows_in[place, 1] = (row_weight * cotan[...].astype(jnp.float32)).astype(jnp.bfloat16)
    send_both(1)
    for m in range(3):
        sibling_copy(m).start()

    def pass_on(distance, kind):
        @pl.when((place - distance >= 0) & has_right)
        def _():
            gather_copy(place - distance, kind, 1).wait_recv()
            gather_copy(place - distance, kind, 1).start()

        @pl.when((place + distance < line) & has_left)
        def _():
            gather_copy(place + distance, kind, 0).wait_recv()
            gather_copy(place + distance, kind, 0).start()

    relays = [(d, kind) for d in range(1, line - 1) for kind in range(2)]
    pieces = [(m, i) for m in range(3) for i in range(PARTS_OF_WEIGHT)]
    for step, (m, i) in enumerate(pieces):
        side_copy(m, i).wait_recv()
        cross_copy(m, i, group).start()
        relay_copy(m, i, 0).start()
        if step % 2 == 1 and relays:
            pass_on(*relays.pop(0))
        if step >= 1:
            mm, ii = pieces[step - 1]
            cross_copy(mm, ii, 1 - group).wait_recv()
            relay_copy(mm, ii, 1).start()
    mm, ii = pieces[-1]
    cross_copy(mm, ii, 1 - group).wait_recv()
    relay_copy(mm, ii, 1).start()
    while relays:
        pass_on(*relays.pop(0))
    for m in range(3):
        own[2 + m].wait()
        sibling_copy(m).wait_recv()
        for i in range(PARTS_OF_WEIGHT):
            relay_copy(m, i, 0).wait_recv()
            relay_copy(m, i, 1).wait_recv()

    contract = (((1,), (1,)), ((), ()))

    def terms(blocks, ready):
        def first(t, _):
            cols = pl.ds(pl.multiple_of(t * 256, 256), 256)
            inputs = jnp.concatenate([rows_in[b, 0] for b in blocks], axis=0)
            scaled = jnp.concatenate([rows_in[b, 1] for b in blocks], axis=0)
            gate = jnp.dot(inputs, weights[0, :, cols], preferred_element_type=jnp.float32)
            upward = jnp.dot(inputs, weights[1, :, cols], preferred_element_type=jnp.float32)
            grad_hidden = jnp.dot(scaled, weights[2, :, cols], preferred_element_type=jnp.float32)
            sigma = jax.nn.sigmoid(gate)
            active = gate * sigma
            hidden[0, :, cols] = (active * upward).astype(jnp.bfloat16)
            hidden[1, :, cols] = (
                grad_hidden * upward * sigma * (1.0 + gate * (1.0 - sigma))
            ).astype(jnp.bfloat16)
            hidden[2, :, cols] = (grad_hidden * active).astype(jnp.bfloat16)
            return 0

        lax.fori_loop(0, weights.shape[2] // 256, first, 0)

        def keep(kind, cols, value):
            for i, b in enumerate(blocks):
                sums[b, kind, :, cols] = value[i * half:(i + 1) * half].astype(jnp.bfloat16)

        def output_tile(t, _):
            cols = pl.ds(pl.multiple_of(t * 512, 512), 512)
            keep(0, cols, lax.dot_general(
                hidden[0], weights[2, cols, :], contract, preferred_element_type=jnp.float32
            ))
            return 0

        lax.fori_loop(0, width // 512, output_tile, 0)
        ready(0)

        def input_tile(t, _):
            cols = pl.ds(pl.multiple_of(t * 512, 512), 512)
            keep(1, cols, lax.dot_general(
                hidden[1], weights[0, cols, :], contract, preferred_element_type=jnp.float32
            ) + lax.dot_general(
                hidden[2], weights[1, cols, :], contract, preferred_element_type=jnp.float32
            ))
            return 0

        lax.fori_loop(0, width // 512, input_tile, 0)
        ready(1)

    def sum_copy(block, kind, part, way):
        cols = pl.ds(part * chunk, chunk)
        return remote(
            sums.at[block, kind, :, cols], arrived.at[way, block, kind, :, cols],
            sums_send.at[block, kind, part], sums_recv.at[way, block, kind, part],
            {"loop": loop + 4 * way - 2},
        )

    quarters = [(kind, part) for kind in range(2) for part in range(2)]
    low = place < line // 2
    at_end = jnp.logical_not(has_left & has_right)
    depth = jnp.where(low, place, line - 1 - place)
    onward_way = jnp.where(low, 1, 0)

    def mirrored(block):
        return jnp.where(low, block, line - 1 - block)

    def forward(block, kind, part, way):
        cols = pl.ds(part * chunk, chunk)
        sum_copy(block, kind, part, way).wait_recv()
        sums[block, kind, :, cols] = (
            sums[block, kind, :, cols].astype(jnp.float32)
            + arrived[way, block, kind, :, cols].astype(jnp.float32)
        ).astype(jnp.bfloat16)
        sum_copy(block, kind, part, way).start()

    def two_blocks(index, _):
        ahead = mirrored(jnp.where(index == 0, 2, 3 - 3 * depth))
        behind = mirrored(jnp.where(index == 0, 1 + 2 * depth, depth))

        @pl.when(at_end)
        def _():
            for kind in range(2):
                gather_copy(ahead, kind, 0).wait_recv()

        @pl.when(at_end & (index == 0))
        def _():
            for kind in range(2):
                gather_copy(behind, kind, 0).wait_recv()

        def ready(kind):
            @pl.when(at_end)
            def _():
                for part in range(2):
                    sum_copy(ahead, kind, part, onward_way).start()

        terms((ahead, behind), ready)

        @pl.when(at_end & (index == 1))
        def _():
            for kind, part in quarters:
                sum_copy(mirrored(1), kind, part, onward_way).start()

        @pl.when(jnp.logical_not(at_end))
        def _():
            for part in range(2):
                forward(mirrored(2), index, part, onward_way)

        return 0

    lax.fori_loop(0, 2, two_blocks, 0)

    @pl.when(jnp.logical_not(at_end))
    def _():
        for step in range(len(quarters) + 1):
            if step < len(quarters):
                forward(mirrored(3), *quarters[step], onward_way)
            if step >= 1:
                forward(mirrored(0), *quarters[step - 1], 1 - onward_way)

    outputs = (mixed_ref, grad_ref)

    def swap_copy(kind):
        return remote(
            swap_out.at[kind], swap_in.at[kind], swap_send.at[kind], swap_recv.at[kind], sibling
        )

    for kind in range(2):
        for part in range(2):
            cols = pl.ds(part * chunk, chunk)
            total[...] = sums[place, kind, :, cols].astype(jnp.float32)

            @pl.when(has_left)
            def _():
                sum_copy(place, kind, part, 1).wait_recv()
                total[...] += arrived[1, place, kind, :, cols].astype(jnp.float32)

            @pl.when(has_right)
            def _():
                sum_copy(place, kind, part, 0).wait_recv()
                total[...] += arrived[0, place, kind, :, cols].astype(jnp.float32)

            value = total[...]
            if kind == 0:
                value = row_weight * value
            value = value.astype(jnp.bfloat16)

            @pl.when(core == part)
            def _():
                outputs[kind][my_rows, :] = value

            @pl.when(core != part)
            def _():
                swap_out[kind] = value
        swap_copy(kind).start()
    other_rows = pl.ds(pl.multiple_of((1 - core) * half, half), half)
    for kind in range(2):
        swap_copy(kind).wait_recv()
        outputs[kind][other_rows, :] = swap_in[kind]

    for kind in range(2):
        swap_copy(kind).wait_send()
    for m in range(3):
        sibling_copy(m).wait_send()
        for i in range(PARTS_OF_WEIGHT):
            side_copy(m, i).wait_send()
            cross_copy(m, i, group).wait_send()
            relay_copy(m, i, 0).wait_send()
            relay_copy(m, i, 1).wait_send()

    def settle(block, _):
        @pl.when(has_left & (block >= place))
        def _():
            for kind in range(2):
                gather_copy(block, kind, 0).wait_send()

        @pl.when(has_right & (block <= place))
        def _():
            for kind in range(2):
                gather_copy(block, kind, 1).wait_send()

        @pl.when(block != place)
        def _():
            for kind, part in quarters:
                sum_copy(block, kind, part, 0).wait_send()
        return 0

    lax.fori_loop(0, line, settle, 0)


def on_line(tokens, cotangent, route_ids, combine, w_gate, w_up, w_down_t):
    rows, width = tokens.shape
    units = w_gate.shape[1]
    half = rows // 2
    line = lax.axis_size("loop") // 2
    any_space = pl.BlockSpec(memory_space=pltpu.HBM)
    vmem = pl.BlockSpec(memory_space=pltpu.VMEM)
    bf16 = jnp.bfloat16
    dma = pltpu.SemaphoreType.DMA
    pieces = PARTS_OF_WEIGHT
    out = jax.ShapeDtypeStruct((rows, width // 2), bf16)
    return pl.pallas_call(
        functools.partial(line_kernel, line),
        out_shape=(out, out),
        in_specs=[pl.BlockSpec(memory_space=pltpu.SMEM), vmem] + [any_space] * 5,
        out_specs=(vmem, vmem),
        scratch_shapes=[
            pltpu.VMEM((3, width, 4 * units), bf16),
            pltpu.VMEM((line, 2, half, width), bf16),
            pltpu.VMEM((half, width), bf16),
            pltpu.VMEM((3, 2 * half, 4 * units), bf16),
            pltpu.VMEM((line, 2, half, width), bf16),
            pltpu.VMEM((2, line, 2, half, width), bf16),
            pltpu.VMEM((half, width // 2), jnp.float32),
            pltpu.VMEM((2, half, width // 2), bf16),
            pltpu.VMEM((2, half, width // 2), bf16),
            dma((5,)),
            dma((2, line, 2)),
            dma((line, 2)),
            dma((3,)),
            dma((3,)),
            dma((3, pieces)),
            dma((3, pieces)),
            dma((3, pieces)),
            dma((3, pieces)),
            dma((2, 3, pieces)),
            dma((2, 3, pieces)),
            dma((line, 2, 2)),
            dma((2, line, 2, 2)),
            dma((2,)),
            dma((2,)),
        ],
        compiler_params=pltpu.CompilerParams(
            collective_id=0, has_side_effects=True, vmem_limit_bytes=62 * 1024 * 1024
        ),
        cost_estimate=pl.CostEstimate(
            flops=12 * line * half * width * 4 * units,
            bytes_accessed=2 * (3 * width * units + 3 * rows * width),
            transcendentals=line * half * 4 * units,
        ),
    )(route_ids, combine.reshape(1, rows), tokens, cotangent, w_gate, w_up, w_down_t)


def from_partner(block, axis, distance):
    count = lax.axis_size(axis)
    route = []
    for low in range(count):
        high = low | 1 << distance
        if high != low and high < count:
            route += [(low, high), (high, low)]
    return lax.ppermute(block, axis, route)


def from_behind(block, axis, distance):
    devices = range(lax.axis_size(axis))
    route = [((i - distance) % len(devices), i) for i in devices]
    return lax.ppermute(block, axis, route)


def block_terms(stacked_weights, group_rows, routed_group, totals):
    weight_gate = stacked_weights[0]
    weight_up = stacked_weights[1]
    weight_down = stacked_weights[2]
    contract = (((1,), (1,)), ((), ()))

    def one_block(position, state):

        def compute(current):
            start = position * BLOCK
            inputs = lax.dynamic_slice_in_dim(group_rows[0], start, BLOCK, 0)
            scaled = lax.dynamic_slice_in_dim(group_rows[1], start, BLOCK, 0)
            gate = jnp.dot(inputs, weight_gate, preferred_element_type=jnp.float32)
            upward = jnp.dot(inputs, weight_up, preferred_element_type=jnp.float32)
            sigma = jax.nn.sigmoid(gate)
            active = gate * sigma
            hidden = (active * upward).astype(jnp.bfloat16)
            output_part = lax.dot_general(
                hidden, weight_down, contract, preferred_element_type=jnp.float32
            )
            grad_hidden = jnp.dot(scaled, weight_down, preferred_element_type=jnp.float32)
            grad_gate = (grad_hidden * upward * sigma * (1.0 + gate * (1.0 - sigma))).astype(
                jnp.bfloat16
            )
            grad_up = (grad_hidden * active).astype(jnp.bfloat16)
            input_part = lax.dot_general(
                grad_gate, weight_gate, contract, preferred_element_type=jnp.float32
            )
            input_part = input_part + lax.dot_general(
                grad_up, weight_up, contract, preferred_element_type=jnp.float32
            )
            previous = lax.dynamic_slice_in_dim(current, start, BLOCK, 1)
            return lax.dynamic_update_slice_in_dim(
                current, previous + jnp.stack([output_part, input_part]), start, 1
            )

        def keep_state(current):
            return current

        return lax.cond(routed_group[position] > 0, compute, keep_state, state)

    return lax.fori_loop(0, routed_group.shape[0], one_block, totals)


def split_halves(values, loop_index, bit):
    half_rows = values.shape[1] // 2
    upper_bit = loop_index >> bit & 1
    lower_part = values[:, :half_rows]
    upper_part = values[:, half_rows:]
    kept = jnp.where(upper_bit == 0, lower_part, upper_part)
    outgoing = jnp.where(upper_bit == 0, upper_part, lower_part)
    return (kept, outgoing)


def on_device(tokens, cotangent, route_ids, combine, w_gate, w_up, w_down_t):
    row_count = tokens.shape[0]
    blocks_here = row_count // BLOCK
    loop_index = lax.axis_index("loop")
    cycle_size = lax.axis_size("loop")
    routed = jnp.any(route_ids == 0, axis=1).astype(jnp.int32)
    local_routed = lax.dynamic_slice_in_dim(routed, loop_index * blocks_here, blocks_here)
    row_weight = combine * jnp.repeat(local_routed.astype(jnp.float32), BLOCK)
    scaled = (row_weight[:, None] * cotangent.astype(jnp.float32)).astype(jnp.bfloat16)
    group_rows = jnp.stack([tokens, scaled])
    for bit in range(2):
        partner = from_partner(group_rows, "loop", bit)
        upper_bit = loop_index >> bit & 1
        group_rows = jnp.where(
            upper_bit == 0,
            jnp.concatenate([group_rows, partner], 1),
            jnp.concatenate([partner, group_rows], 1),
        )
    group_start = loop_index // 4 * 4 * blocks_here
    routed_group = lax.dynamic_slice_in_dim(routed, group_start, 4 * blocks_here)
    totals = jnp.zeros((2, 4 * row_count, tokens.shape[1]), jnp.float32)
    weights = jnp.stack([w_gate, w_up, w_down_t])
    turns = cycle_size // 4

    def turn_once(step, carry):
        current, sums = carry
        sums = block_terms(current, group_rows, routed_group, sums)
        current = from_behind(current, "loop", 4)
        return (current, sums)

    weights, totals = lax.fori_loop(0, turns - 1, turn_once, (weights, totals))
    totals = block_terms(weights, group_rows, routed_group, totals)
    rounded = totals.astype(jnp.bfloat16)
    kept, outgoing = split_halves(rounded, loop_index, 1)
    received = from_partner(outgoing, "loop", 1)
    sums = kept.astype(jnp.float32) + received.astype(jnp.float32)
    kept, outgoing = split_halves(sums, loop_index, 0)
    sums = kept + from_partner(outgoing.astype(jnp.bfloat16), "loop", 0).astype(outgoing.dtype)
    sums = lax.psum_scatter(
        sums.astype(jnp.bfloat16), "hid", scatter_dimension=2, tiled=True
    ).astype(jnp.float32)
    mixed = (row_weight[:, None] * sums[0]).astype(jnp.bfloat16)
    tokens_grad = sums[1].astype(jnp.bfloat16)
    return (mixed, tokens_grad)


def solution(mesh):
    in_specs = (
        P(("groups", "loop"), None),
        P(("groups", "loop"), None),
        P("groups", None),
        P(("groups", "loop")),
        P(None, ("loop", "hid")),
        P(None, ("loop", "hid")),
        P(None, ("loop", "hid")),
    )
    out_specs = (P(("groups", "loop"), "hid"), P(("groups", "loop"), "hid"))
    sizes = dict(mesh.shape)
    short = sizes["groups"] == 2 and sizes["hid"] == 2 and sizes["loop"] == 8
    return jax.shard_map(
        on_line if short else on_device, mesh=mesh, in_specs=in_specs, out_specs=out_specs, check_vma=False
    )
```
